512 devices in a mesh: batch: 128 (over y, z, core), width: 4 (over x).
Axes of the slice: x: 4, y: 4, z: 16, core: 2. Of those that a mesh axis runs over, the one named last changes fastest.
Arguments:
- teacher: bfloat16 [32768, 4096], P('batch', 'width'), may hold values from -48 to 48, as said below
- student: bfloat16 [32768, 1024], P('batch', 'width'), may hold values from -48 to 48, as said below
Outputs:
- grad: float32 [32768, 1024], P('batch', 'width')
The draws below stay inside these ranges and needn't reach their ends.
Inputs may be any that keep to these rules, and one draw needn't show every extreme that they name: `teacher`: Real-valued embeddings. `student`: Real-valued embeddings.
All inputs are finite; a program needn't handle non-finite values.
Results may differ from the reference program's by a relative error of at most 0.00075.
Values may be sent and summed in bfloat16 or wider, within the bound.
A program may use at most 64 MiB of HBM per device.

```python
import math
import jax
import jax.numpy as jnp
from jax import lax

DT = 4096
DS = 1024
ROWS_DEV = 256
REACH = 4
ROWS = 32768
NEAR = 2304
N_BATCH = 128


def row_scales(key):
    place = jnp.arange(ROWS, dtype=jnp.float32) / max(ROWS - 1, 1)
    spread = jax.random.uniform(jax.random.fold_in(key, 5), (ROWS, 1), minval=math.log(1.2), maxval=math.log(4.8))
    return jnp.exp(spread) * (0.5 + place[:, None])


def draw_teacher(key, part):
    scales = row_scales(key)
    second = jax.random.fold_in(jax.random.fold_in(key, 11), 0)
    values = scales * jnp.clip(jax.random.normal(second, (ROWS, DT)), -6.0, 6.0)
    return values.astype(jnp.bfloat16)


def draw_student(key, part):
    scales = row_scales(key)
    second = jax.random.fold_in(jax.random.fold_in(key, 23), 0)
    values = scales * jnp.clip(jax.random.normal(second, (ROWS, DS)), -6.0, 6.0)
    return values.astype(jnp.bfloat16)


def setup_inputs(seed: int = 0) -> dict:
    splits = jax.random.split(jax.random.key(seed), 3)
    teacher = draw_teacher(jax.random.fold_in(splits[2], 71), 0)
    student = draw_student(jax.random.fold_in(splits[2], 71), 0)
    return dict(teacher=teacher, student=student)


def reference(teacher, student):
    teacher_wide = teacher.astype(jnp.float32)
    student_wide = student.astype(jnp.float32)
    teacher_sq = jnp.sum(teacher_wide * teacher_wide, axis=1) / DT
    student_sq = jnp.sum(student_wide * student_wide, axis=1) / DS
    width_band = 2 * REACH + 1
    teacher_blocks = jnp.pad(teacher_wide.reshape(N_BATCH, ROWS_DEV, DT), ((REACH, REACH), (0, 0), (0, 0)))
    student_blocks = jnp.pad(student_wide.reshape(N_BATCH, ROWS_DEV, DS), ((REACH, REACH), (0, 0), (0, 0)))
    student_lowpad = jnp.pad(student.reshape(N_BATCH, ROWS_DEV, DS), ((REACH, REACH), (0, 0), (0, 0)))
    tsq_blocks = jnp.pad(teacher_sq.reshape(N_BATCH, ROWS_DEV), ((REACH, REACH), (0, 0)))
    ssq_blocks = jnp.pad(student_sq.reshape(N_BATCH, ROWS_DEV), ((REACH, REACH), (0, 0)))
    offsets = jnp.arange(width_band, dtype=jnp.int32) - REACH

    def one(block):
        start = block.astype(jnp.int32)
        own_t = lax.dynamic_index_in_dim(teacher_blocks, start + REACH, 0, keepdims=False)
        own_s = lax.dynamic_index_in_dim(student_blocks, start + REACH, 0, keepdims=False)
        own_tsq = lax.dynamic_index_in_dim(tsq_blocks, start + REACH, 0, keepdims=False)
        own_ssq = lax.dynamic_index_in_dim(ssq_blocks, start + REACH, 0, keepdims=False)
        win_t = lax.dynamic_slice_in_dim(teacher_blocks, start, width_band, 0).reshape(NEAR, DT)
        win_s = lax.dynamic_slice_in_dim(student_blocks, start, width_band, 0).reshape(NEAR, DS)
        win_low = lax.dynamic_slice_in_dim(student_lowpad, start, width_band, 0).reshape(NEAR, DS)
        win_tsq = lax.dynamic_slice_in_dim(tsq_blocks, start, width_band, 0).reshape(NEAR)
        win_ssq = lax.dynamic_slice_in_dim(ssq_blocks, start, width_band, 0).reshape(NEAR)
        tgram = jnp.dot(own_t, win_t.T, precision=lax.Precision.HIGHEST)
        sgram = jnp.dot(own_s, win_s.T, precision=lax.Precision.HIGHEST)
        sdist = own_ssq[:, None] + win_ssq[None, :] - 2.0 * sgram / DS
        tdist = own_tsq[:, None] + win_tsq[None, :] - 2.0 * tgram / DT
        partner = start + offsets
        valid = jnp.logical_and(partner >= 0, partner < N_BATCH)
        valid_cols = jnp.repeat(valid, ROWS_DEV)
        residual = jnp.where(valid_cols[None, :], sdist - tdist, jnp.zeros_like(sdist))
        row_total = jnp.sum(residual, axis=1)
        residual_low = residual.astype(jnp.bfloat16)
        pulled = jnp.dot(residual_low, win_low, preferred_element_type=jnp.float32)
        return (own_s * row_total[:, None] - pulled) / NEAR

    grads = lax.map(one, jnp.arange(N_BATCH, dtype=jnp.int32))
    return grads.reshape(ROWS, DS)
```

```python
import functools

import jax
import jax.numpy as jnp
from jax import lax
from jax.experimental import pallas as pl
from jax.experimental.pallas import tpu as pltpu
from jax.sharding import PartitionSpec as P

DT = 4096
DS = 1024
REACH = 4
MESH = pl.DeviceIdType.MESH
CHUNKS = 4
F32 = jnp.float32
BF16 = jnp.bfloat16


def dot(a, b, ca, cb):
    return lax.dot_general(a, b, (((ca,), (cb,)), ((), ())), preferred_element_type=F32)


def kernel(
    batch, width, rows, ks, kt, n,
    t_ref, s_ref, o_ref,
    bbuf, abuf, cbuf, eself, rself, esend, erecv, eselfrecv, rfull,
    acc_a, acc_b, acc_c, msg_c, msg_a, msg_d, got_c, got_a, got_d, hb,
    in_sem, up_send, down_send, a_recv, c_recv, fwd_send, fwd_recv, b_send, b_recv,
    rs_send, rs_recv, ag_send, ag_recv, m_send, m_recv,
):
    k_all = ks + kt
    part = rows // n
    piece = part // width
    me = lax.axis_index("batch")
    wx = lax.axis_index("width")
    core = lax.rem(me, 2)
    chip = me // 2
    has_prev = chip > 0
    has_next = chip < batch // 2 - 1
    prev = (lax.rem(me + batch - 2, batch), wx)
    nxt = (lax.rem(me + 2, batch), wx)
    other = 1 - core
    mate = (me + 1 - 2 * core, wx)

    def peer(d):
        return lax.rem(wx + d, width)

    barrier = pltpu.get_barrier_semaphore()

    def greet(device):
        pl.semaphore_signal(barrier, inc=1, device_id=device, device_id_type=MESH)

    greet(mate)
    for d in range(1, width):
        greet((me, peer(d)))

    @pl.when(has_prev)
    def _():
        greet(prev)

    @pl.when(has_next)
    def _():
        greet(nxt)

    loads = [
        pltpu.make_async_copy(s_ref, bbuf.at[core, :, pl.ds(0, ks)], in_sem.at[0]),
        pltpu.make_async_copy(t_ref, bbuf.at[core, :, pl.ds(ks, kt)], in_sem.at[1]),
    ]
    for c in loads:
        c.start()

    @pl.when(jnp.logical_not(has_prev))
    def _():
        abuf[...] = jnp.zeros_like(abuf)

    @pl.when(jnp.logical_not(has_next))
    def _():
        cbuf[...] = jnp.zeros_like(cbuf)

    for c in loads:
        c.wait()

    pl.semaphore_wait(barrier, width + has_prev.astype(jnp.int32) + has_next.astype(jnp.int32))

    def remote(src, dst, send, recv, device):
        return pltpu.make_async_remote_copy(
            src_ref=src, dst_ref=dst, send_sem=send, recv_sem=recv, device_id=device, device_id_type=MESH
        )

    def own(q):
        return bbuf.at[core, pl.ds(q * part, part)]

    ups = [remote(own(q), abuf.at[q, core], up_send.at[q], a_recv.at[q], nxt) for q in range(n)]
    downs = [remote(own(q), cbuf.at[q], down_send.at[q], c_recv.at[q], prev) for q in range(n)]
    fwds = [remote(abuf.at[q, core], abuf.at[q, core], fwd_send.at[q], fwd_recv.at[q], mate) for q in range(n)]
    share = remote(bbuf.at[core], bbuf.at[core], b_send, b_recv, mate)
    share.start()
    for q in range(n):
        @pl.when(has_next)
        def _(q=q):
            ups[q].start()

        @pl.when(has_prev)
        def _(q=q):
            downs[q].start()

    lane = lax.broadcasted_iota(jnp.int32, (1, k_all), 1)
    signs = jnp.where(lane < ks, -float(DT // DS), 1.0).astype(F32)
    signs_low = signs.astype(BF16)

    def half_norm(x):
        wide = x.astype(F32)
        return 0.5 * jnp.sum(wide * wide * signs, axis=1, keepdims=True)

    def as_row(col):
        m = col.shape[0]
        pieces = [
            jnp.transpose(jnp.broadcast_to(col[i : i + 128], (128, 128)))[0:1, :] for i in range(0, m, 128)
        ]
        return pieces[0] if len(pieces) == 1 else jnp.concatenate(pieces, axis=1)

    scale = 2.0 / DT
    ones = jnp.ones((1, 128), BF16)

    def aug(s):
        return jnp.concatenate([s, jnp.broadcast_to(ones, (s.shape[0], 128))], axis=1)

    widths = [2 * rows] + [2 * rows + 2 * part * (q + 1) + 2 * part * q for q in range(n)]

    def scatter(stage, src, dst):
        cs = [
            remote(src.at[peer(d)], dst.at[d - 1], rs_send.at[stage, d - 1], rs_recv.at[stage, d - 1], (me, peer(d)))
            for d in range(1, width)
        ]
        for c in cs:
            c.start()
        return cs

    def reduce(cs, src, dst, mask):
        total = src[wx].astype(F32)
        for c in cs:
            c.wait_recv()
        for d in range(width - 1):
            total = total + dst[d].astype(F32)
        if mask is not None:
            total = jnp.where(mask, total, 0.0)
        return total.astype(BF16)

    def gather(stage, out, low):
        out[wx] = low
        cs = [
            remote(out.at[wx], out.at[wx], ag_send.at[stage, d - 1], ag_recv.at[stage, d - 1], (me, peer(d)))
            for d in range(1, width)
        ]
        for c in cs:
            c.start()
        return cs

    share.wait_recv()
    for i in range(2):
        hb[:, i * rows : (i + 1) * rows] = as_row(half_norm(bbuf[i]))
    mine = bbuf[core]
    g = dot(mine * signs_low, bbuf[...].reshape(2 * rows, k_all), 1, 1)
    e = (g - half_norm(mine) - hb[...]) * scale
    eself[...] = e.astype(BF16).reshape(width, rows // width, 2 * rows)
    scatters = [scatter(0, eself, eselfrecv)]
    gathers = [None] * (n + 1)

    acc_a[...] = jnp.zeros_like(acc_a)
    acc_b[...] = jnp.zeros_like(acc_b)
    acc_c[...] = jnp.zeros_like(acc_c)
    gathers[0] = gather(0, rself, reduce(scatters[0], eself, eselfrecv, None))

    def pull(stage):
        for c in gathers[stage]:
            c.wait_recv()
        sb = aug(bbuf[:, :, 0:ks].reshape(2 * rows, ks))
        if stage == 0:
            r = rself[...].reshape(rows, 2 * rows)
            acc_b[core] += dot(r, sb, 1, 0)
            return
        q = stage - 1
        r = rfull[q, :, :, 0 : widths[stage]].reshape(part, widths[stage])
        sc = aug(cbuf[q, :, 0:ks])
        sa = aug(abuf[0 : q + 1, :, :, 0:ks].reshape(2 * part * (q + 1), ks))
        rb = r[:, 0 : 2 * rows]
        ra = r[:, 2 * rows : 2 * rows + 2 * part * (q + 1)]
        acc_c[q] += dot(rb, sb, 1, 0) + dot(ra, sa, 1, 0)
        acc_b[...] += dot(rb, sc, 0, 0).reshape(2, rows, ks + 128)
        acc_a[0 : q + 1] += dot(ra, sc, 0, 0).reshape(q + 1, 2, part, ks + 128)
        sa_q = aug(abuf[q, :, :, 0:ks].reshape(2 * part, ks))
        for p in range(q):
            at = 2 * rows + 2 * part * (q + 1 + p)
            rp = r[:, at : at + 2 * part]
            acc_c[p] += dot(rp, sa_q, 1, 0)
            acc_a[q] += dot(rp, aug(cbuf[p, :, 0:ks]), 0, 0).reshape(2, part, ks + 128)

    half_c = []
    half_a = []
    for q in range(n):
        stage = 1 + q

        @pl.when(has_prev)
        def _(q=q):
            ups[q].wait_recv()
            fwds[q].start()

        @pl.when(has_next)
        def _(q=q):
            downs[q].wait_recv()

        @pl.when(has_prev)
        def _(q=q):
            fwds[q].wait_recv()

        c_low = cbuf[q]
        c_scaled = c_low * signs_low
        a_q = abuf[q].reshape(2 * part, k_all)
        half_c.append(half_norm(c_low))
        half_a.append(as_row(half_norm(a_q)))
        gb = dot(c_scaled, bbuf[...].reshape(2 * rows, k_all), 1, 1)
        ga = dot(c_scaled, abuf[0 : q + 1].reshape(2 * part * (q + 1), k_all), 1, 1)
        cols = [(gb - half_c[q] - hb[...])]
        cols.append(ga - half_c[q] - (half_a[0] if q == 0 else jnp.concatenate(half_a, axis=1)))
        for p in range(q):
            gp = dot(cbuf[p] * signs_low, a_q, 1, 1)
            cols.append(gp - half_c[p] - half_a[q])
        at = 0
        for col in cols:
            wide = col.shape[1]
            esend[q, :, :, at : at + wide] = (col * scale).astype(BF16).reshape(width, piece, wide)
            at += wide
        view = lambda ref, q=q: ref.at[q, :, :, pl.ds(0, widths[1 + q])]
        scatters.append(scatter(stage, view(esend), view(erecv)))
        pull(stage - 1)
        lanes = lax.broadcasted_iota(jnp.int32, (1, widths[stage]), 1)
        in_a = lanes >= 2 * rows
        first = lax.rem(lanes // part, 2) == 0
        skip = jnp.logical_and(in_a, jnp.logical_or(jnp.logical_not(has_prev), jnp.logical_and(first, core == 1)))
        mask = jnp.logical_and(has_next, jnp.logical_not(skip))
        low = reduce(scatters[stage], view(esend), view(erecv), mask)
        gathers[stage] = gather(stage, view(rfull), low)
    pull(n)

    def message(s, acc):
        total = acc[:, ks : ks + 128]
        wide = s.astype(F32)
        return jnp.concatenate([wide[:, i : i + 128] * total for i in range(0, ks, 128)], axis=1) - acc[:, 0:ks]

    msg_c[...] = message(cbuf[:, :, 0:ks].reshape(rows, ks), acc_c[...].reshape(rows, ks + 128))
    send_c = remote(msg_c, got_c, m_send.at[0], m_recv.at[0], nxt)

    @pl.when(has_next)
    def _():
        send_c.start()

    msg_d[0] = message(abuf[:, other, :, 0:ks].reshape(rows, ks), acc_a[:, other].reshape(rows, ks + 128))
    msg_d[1] = message(bbuf[other, :, 0:ks], acc_b[other])
    send_d = remote(msg_d, got_d, m_send.at[1], m_recv.at[1], mate)
    send_d.start()
    mine_a = message(abuf[:, core, :, 0:ks].reshape(rows, ks), acc_a[:, core].reshape(rows, ks + 128))
    send_d.wait_recv()
    msg_a[...] = mine_a + got_d[0]
    send_a = remote(msg_a, got_a, m_send.at[2], m_recv.at[2], prev)

    @pl.when(has_prev)
    def _():
        send_a.start()

    near = (2 * REACH + 1) * rows
    o_ref[...] = message(bbuf[core, :, 0:ks], acc_b[core]) + got_d[1]

    @pl.when(has_prev)
    def _():
        send_c.wait_recv()
        o_ref[...] += got_c[...]

    @pl.when(has_next)
    def _():
        send_a.wait_recv()
        o_ref[...] += got_a[...]

    o_ref[...] = o_ref[...] / near

    share.wait_send()
    send_d.wait_send()
    for cs in scatters + gathers:
        for c in cs:
            c.wait_send()

    @pl.when(has_next)
    def _():
        for c in ups:
            c.wait_send()
        send_c.wait_send()

    @pl.when(has_prev)
    def _():
        for c in downs + fwds:
            c.wait_send()
        send_a.wait_send()


def solution(mesh):
    batch, width = mesh.shape["batch"], mesh.shape["width"]
    n = CHUNKS

    def body(teacher, student):
        rows, kt = teacher.shape
        ks = student.shape[1]
        part = rows // n
        k_all = ks + kt
        wide = 2 * rows + 2 * part * (2 * n - 1)
        dma = pltpu.SemaphoreType.DMA
        return pl.pallas_call(
            functools.partial(kernel, batch, width, rows, ks, kt, n),
            out_shape=jax.ShapeDtypeStruct((rows, ks), F32),
            in_specs=[pl.BlockSpec(memory_space=pl.ANY)] * 2,
            out_specs=pl.BlockSpec(memory_space=pltpu.VMEM),
            scratch_shapes=[
                pltpu.VMEM((2, rows, k_all), BF16),
                pltpu.VMEM((n, 2, part, k_all), BF16),
                pltpu.VMEM((n, part, k_all), BF16),
                pltpu.VMEM((width, rows // width, 2 * rows), BF16),
                pltpu.VMEM((width, rows // width, 2 * rows), BF16),
                pltpu.VMEM((n, width, part // width, wide), BF16),
                pltpu.VMEM((n, width - 1, part // width, wide), BF16),
                pltpu.VMEM((width - 1, rows // width, 2 * rows), BF16),
                pltpu.VMEM((n, width, part // width, wide), BF16),
                pltpu.VMEM((n, 2, part, ks + 128), F32),
                pltpu.VMEM((2, rows, ks + 128), F32),
                pltpu.VMEM((n, part, ks + 128), F32),
                pltpu.VMEM((rows, ks), F32),
                pltpu.VMEM((rows, ks), F32),
                pltpu.VMEM((2, rows, ks), F32),
                pltpu.VMEM((rows, ks), F32),
                pltpu.VMEM((rows, ks), F32),
                pltpu.VMEM((2, rows, ks), F32),
                pltpu.VMEM((1, 2 * rows), F32),
                dma((2,)), dma((n,)), dma((n,)), dma((n,)), dma((n,)), dma((n,)), dma((n,)), dma, dma,
                dma((n + 1, width - 1)), dma((n + 1, width - 1)), dma((n + 1, width - 1)), dma((n + 1, width - 1)),
                dma((3,)), dma((3,)),
            ],
            compiler_params=pltpu.CompilerParams(
                collective_id=0, has_side_effects=True, vmem_limit_bytes=40 * 2**20
            ),
        )(teacher, student)

    specs = (P("batch", "width"), P("batch", "width"))
    return jax.shard_map(body, mesh=mesh, in_specs=specs, out_specs=P("batch", "width"), check_vma=False)
```

```python
import functools

import jax
import jax.numpy as jnp
from jax import lax
from jax.experimental import pallas as pl
from jax.experimental.pallas import tpu as pltpu
from jax.sharding import PartitionSpec as P

DT = 4096
DS = 1024
REACH = 4
MESH = pl.DeviceIdType.MESH
CHUNKS = 4
F32 = jnp.float32
BF16 = jnp.bfloat16


def dot(a, b, ca, cb):
    return lax.dot_general(a, b, (((ca,), (cb,)), ((), ())), preferred_element_type=F32)


def kernel(
    batch, width, rows, ks, kt, n,
    t_ref, s_ref, o_ref,
    bbuf, abuf, cbuf, eself, rself, esend, erecv, eselfrecv, rfull,
    acc_a, acc_b, acc_c, sum_a, sum_b, sum_c, sum_own,
    msg_c, msg_a, msg_d, msum_c, msum_a, msum_d,
    got_c, got_a, got_a2, got_d, gsum_c, gsum_a, gsum_a2, gsum_d, hb, col_a,
    in_sem, up_send, down_send, a_recv, c_recv, fwd_send, fwd_recv, b_send, b_recv,
    rs_send, rs_recv, ag_send, ag_recv, m_send, m_recv,
):
    k_all = ks + kt
    part = rows // n
    piece = part // width
    me = lax.axis_index("batch")
    wx = lax.axis_index("width")
    core = lax.rem(me, 2)
    chip = me // 2
    has_prev = chip > 0
    has_next = chip < batch // 2 - 1
    prev = (lax.rem(me + batch - 2, batch), wx)
    nxt = (lax.rem(me + 2, batch), wx)
    other = 1 - core
    mate = (me + 1 - 2 * core, wx)
    cross_out = jnp.logical_and(core == 0, has_prev)
    cross_in = jnp.logical_and(core == 1, has_next)
    before = (lax.rem(me + batch - 1, batch), wx)
    after = (lax.rem(me + 1, batch), wx)

    def peer(d):
        return lax.rem(wx + d, width)

    barrier = pltpu.get_barrier_semaphore()

    def greet(device):
        pl.semaphore_signal(barrier, inc=1, device_id=device, device_id_type=MESH)

    @pl.when(has_prev)
    def _():
        greet(prev)

    @pl.when(has_next)
    def _():
        greet(nxt)

    @pl.when(cross_out)
    def _():
        greet(before)

    @pl.when(cross_in)
    def _():
        greet(after)

    for d in range(1, width):
        greet((me, peer(d)))
    greet(mate)

    loads = [
        pltpu.make_async_copy(s_ref, bbuf.at[core, :, pl.ds(0, ks)], in_sem.at[0]),
        pltpu.make_async_copy(t_ref, bbuf.at[core, :, pl.ds(ks, kt)], in_sem.at[1]),
    ]
    for c in loads:
        c.start()

    @pl.when(jnp.logical_not(has_prev))
    def _():
        abuf[...] = jnp.zeros_like(abuf)

    @pl.when(jnp.logical_not(has_next))
    def _():
        cbuf[...] = jnp.zeros_like(cbuf)

    for ref in (acc_a, acc_b, acc_c, sum_a, sum_b, sum_c):
        ref[...] = jnp.zeros_like(ref)

    for c in loads:
        c.wait()

    as_int = lambda x: x.astype(jnp.int32)
    crossing = jnp.logical_or(cross_out, cross_in)
    pl.semaphore_wait(barrier, width + as_int(has_prev) + as_int(has_next) + as_int(crossing))

    def remote(src, dst, send, recv, device):
        return pltpu.make_async_remote_copy(
            src_ref=src, dst_ref=dst, send_sem=send, recv_sem=recv, device_id=device, device_id_type=MESH
        )

    def own(q):
        return bbuf.at[core, pl.ds(q * part, part)]

    ups = [remote(own(q), abuf.at[q, core], up_send.at[q], a_recv.at[q], nxt) for q in range(n)]
    downs = [remote(own(q), cbuf.at[q], down_send.at[q], c_recv.at[q], prev) for q in range(n)]
    fwds = [remote(abuf.at[q, core], abuf.at[q, core], fwd_send.at[q], fwd_recv.at[q], mate) for q in range(n)]
    share = remote(bbuf.at[core], bbuf.at[core], b_send, b_recv, mate)
    share.start()
    for q in range(n):
        @pl.when(has_next)
        def _(q=q):
            ups[q].start()

        @pl.when(has_prev)
        def _(q=q):
            downs[q].start()

    lane = lax.broadcasted_iota(jnp.int32, (1, k_all), 1)
    signs = jnp.where(lane < ks, -float(DT // DS), 1.0).astype(F32)
    signs_low = signs.astype(BF16)

    def half_norm(x):
        wide = x.astype(F32)
        return 0.5 * jnp.sum(wide * wide * signs, axis=1, keepdims=True)

    def as_row(col):
        m = col.shape[0]
        pieces = [
            jnp.transpose(jnp.broadcast_to(col[i : i + 128, 0:1], (128, 128)))[0:1, :] for i in range(0, m, 128)
        ]
        return pieces[0] if len(pieces) == 1 else jnp.concatenate(pieces, axis=1)

    def as_col(row):
        m = row.shape[1]
        pieces = [jnp.transpose(jnp.broadcast_to(row[0:1, i : i + 128], (128, 128))) for i in range(0, m, 128)]
        return pieces[0] if len(pieces) == 1 else jnp.concatenate(pieces, axis=0)

    scale = 2.0 / DT

    widths = [2 * rows] + [2 * rows + 2 * part * (q + 1) + 2 * part * q for q in range(n)]

    def scatter(stage, src, dst):
        cs = [
            remote(src.at[peer(d)], dst.at[d - 1], rs_send.at[stage, d - 1], rs_recv.at[stage, d - 1], (me, peer(d)))
            for d in range(1, width)
        ]
        for c in cs:
            c.start()
        return cs

    def reduce(cs, src, dst, mask):
        total = src[wx].astype(F32)
        for c in cs:
            c.wait_recv()
        for d in range(width - 1):
            total = total + dst[d].astype(F32)
        if mask is not None:
            total = jnp.where(mask, total, 0.0)
        return total.astype(BF16)

    def gather(stage, out, low):
        out[wx] = low
        cs = [
            remote(out.at[wx], out.at[wx], ag_send.at[stage, d - 1], ag_recv.at[stage, d - 1], (me, peer(d)))
            for d in range(1, width)
        ]
        for c in cs:
            c.start()
        return cs

    scatters = [None] * (n + 1)
    gathers = [None] * (n + 1)

    share.wait_recv()
    for i in range(2):
        hb[:, i * rows : (i + 1) * rows] = as_row(half_norm(bbuf[i]))
    mine = bbuf[core]
    g = dot(mine * signs_low, bbuf[...].reshape(2 * rows, k_all), 1, 1)
    e = (g - half_norm(mine) - hb[...]) * scale
    eself[...] = e.astype(BF16).reshape(width, rows // width, 2 * rows)
    scatters[0] = scatter(0, eself, eselfrecv)

    def view(ref, q):
        return ref.at[q, :, :, pl.ds(0, widths[1 + q])]

    def finish(stage):
        if stage == 0:
            gathers[0] = gather(0, rself, reduce(scatters[0], eself, eselfrecv, None))
            return
        q = stage - 1
        lanes = lax.broadcasted_iota(jnp.int32, (1, widths[stage]), 1)
        in_a = lanes >= 2 * rows
        first = lax.rem(lanes // part, 2) == 0
        skip = jnp.logical_and(in_a, jnp.logical_or(jnp.logical_not(has_prev), jnp.logical_and(first, core == 1)))
        mask = jnp.logical_and(has_next, jnp.logical_not(skip))
        low = reduce(scatters[stage], view(esend, q), view(erecv, q), mask)
        gathers[stage] = gather(stage, view(rfull, q), low)

    def row_sum(r):
        return jnp.broadcast_to(jnp.sum(r.astype(F32), axis=1, keepdims=True), (r.shape[0], 128))

    def col_sum(r):
        return jnp.sum(r.astype(F32), axis=0, keepdims=True)

    def pull(stage):
        for c in gathers[stage]:
            c.wait_recv()
        sb = bbuf[:, :, 0:ks].reshape(2 * rows, ks)
        if stage == 0:
            r = rself[...].reshape(rows, 2 * rows)
            acc_b[core] += dot(r, sb, 1, 0)
            sum_own[...] = row_sum(r)
            return
        q = stage - 1
        r = rfull[q, :, :, 0 : widths[stage]].reshape(part, widths[stage])
        sc = cbuf[q, :, 0:ks]
        sa = abuf[0 : q + 1, :, :, 0:ks].reshape(2 * part * (q + 1), ks)
        sa_q = abuf[q, :, :, 0:ks].reshape(2 * part, ks)
        a_end = 2 * rows + 2 * part * (q + 1)
        rb = r[:, 0 : 2 * rows]
        ra = r[:, 2 * rows : a_end]
        rp = [r[:, a_end + 2 * part * p : a_end + 2 * part * (p + 1)] for p in range(q)]
        acc_c[q] += dot(rb, sb, 1, 0) + dot(ra, sa, 1, 0)
        sum_c[q] += row_sum(r[:, 0:a_end])
        for p in range(q):
            acc_c[p] += dot(rp[p], sa_q, 1, 0)
            sum_c[p] += row_sum(rp[p])
        if stage == n:
            send_rows_c()
        acc_a[0 : q + 1] += dot(ra, sc, 0, 0).reshape(q + 1, 2, part, ks)
        sum_a[0:1, 0 : 2 * part * (q + 1)] += col_sum(ra)
        for p in range(q):
            acc_a[q] += dot(rp[p], cbuf[p, :, 0:ks], 0, 0).reshape(2, part, ks)
            sum_a[0:1, 2 * part * q : 2 * part * (q + 1)] += col_sum(rp[p])
        if stage == n:
            send_rows_a()
        acc_b[...] += dot(rb, sc, 0, 0).reshape(2, rows, ks)
        sum_b[0:1] += col_sum(rb)

    def pair(i, src, dst, ssrc, sdst, device):
        return [
            remote(src, dst, m_send.at[2 * i], m_recv.at[2 * i], device),
            remote(ssrc, sdst, m_send.at[2 * i + 1], m_recv.at[2 * i + 1], device),
        ]

    send_c = pair(0, msg_c, got_c, msum_c, gsum_c, nxt)
    send_a = pair(1, msg_a.at[core], got_a, msum_a, gsum_a, prev)
    send_a2 = pair(2, msg_a.at[other], got_a2, msum_a, gsum_a2, before)
    send_d = pair(3, msg_d, got_d, msum_d, gsum_d, mate)

    def send_rows_c():
        msg_c[...] = acc_c[...].reshape(rows, ks).astype(BF16)
        msum_c[...] = jnp.broadcast_to(as_row(sum_c[...].reshape(rows, 128)), (8, rows))

        @pl.when(has_next)
        def _():
            for c in send_c:
                c.start()

    def send_rows_a():
        for i in range(2):
            msg_a[i] = acc_a[:, i].reshape(rows, ks).astype(BF16)
        msum_a[...] = jnp.broadcast_to(sum_a[0:1], (8, 2 * rows))

        @pl.when(has_prev)
        def _():
            for c in send_a:
                c.start()

        @pl.when(cross_out)
        def _():
            for c in send_a2:
                c.start()

    half_c, half_a = [], []
    for q in range(n):
        stage = 1 + q

        @pl.when(has_prev)
        def _(q=q):
            ups[q].wait_recv()
            fwds[q].start()

        @pl.when(has_next)
        def _(q=q):
            downs[q].wait_recv()

        @pl.when(has_prev)
        def _(q=q):
            fwds[q].wait_recv()

        c_low = cbuf[q]
        c_scaled = c_low * signs_low
        a_q = abuf[q].reshape(2 * part, k_all)
        half_c.append(half_norm(c_low))
        half_a.append(as_row(half_norm(a_q)))
        gb = dot(c_scaled, bbuf[...].reshape(2 * rows, k_all), 1, 1)
        ga = dot(c_scaled, abuf[0 : q + 1].reshape(2 * part * (q + 1), k_all), 1, 1)
        cols = [gb - half_c[q] - hb[...]]
        cols.append(ga - half_c[q] - (half_a[0] if q == 0 else jnp.concatenate(half_a, axis=1)))
        for p in range(q):
            gp = dot(cbuf[p] * signs_low, a_q, 1, 1)
            cols.append(gp - half_c[p] - half_a[q])
        at = 0
        for col in cols:
            wide = col.shape[1]
            esend[q, :, :, at : at + wide] = (col * scale).astype(BF16).reshape(width, piece, wide)
            at += wide
        scatters[stage] = scatter(stage, view(esend, q), view(erecv, q))
        finish(stage - 1)
        if q:
            pull(stage - 2)
    finish(n)
    pull(n - 1)
    pull(n)

    msg_d[...] = acc_b[other]
    msum_d[...] = jnp.broadcast_to(sum_b[0:1], (8, 2 * rows))
    for c in send_d:
        c.start()
    mine_b = acc_b[core]
    cols_of = lambda x, i: x[0:1, i * rows : (i + 1) * rows]
    sums = jnp.where(core == 0, cols_of(sum_b, 0), cols_of(sum_b, 1))
    for c in send_d:
        c.wait_recv()
    sums = sums + jnp.where(core == 0, cols_of(gsum_d, 0), cols_of(gsum_d, 1))
    o_ref[...] = mine_b + got_d[...]

    @pl.when(jnp.logical_not(has_prev))
    def _():
        gsum_c[...] = jnp.zeros_like(gsum_c)

    @pl.when(jnp.logical_not(has_next))
    def _():
        gsum_a[...] = jnp.zeros_like(gsum_a)

    @pl.when(jnp.logical_not(cross_in))
    def _():
        gsum_a2[...] = jnp.zeros_like(gsum_a2)

    @pl.when(cross_in)
    def _():
        for c in send_a2:
            c.wait_recv()
        o_ref[...] += got_a2[...].astype(F32)

    @pl.when(has_prev)
    def _():
        for c in send_c:
            c.wait_recv()
        o_ref[...] += got_c[...].astype(F32)

    @pl.when(has_next)
    def _():
        for c in send_a:
            c.wait_recv()
        o_ref[...] += got_a[...].astype(F32)

    sums = sums + gsum_c[0:1]
    col_a[...] = as_col(gsum_a[0:1] + gsum_a2[0:1]).reshape(n, 2, part, 128)
    total = as_col(sums) + col_a[:, core].reshape(rows, 128) + sum_own[...]
    near = (2 * REACH + 1) * rows
    s_own = bbuf[core, :, 0:ks].astype(F32)
    for i in range(0, ks, 128):
        o_ref[:, i : i + 128] = (s_own[:, i : i + 128] * total - o_ref[:, i : i + 128]) * (1.0 / near)

    share.wait_send()
    for c in send_d:
        c.wait_send()
    for cs in scatters + gathers:
        for c in cs:
            c.wait_send()

    @pl.when(has_next)
    def _():
        for c in ups + send_c:
            c.wait_send()

    @pl.when(has_prev)
    def _():
        for c in downs + fwds + send_a:
            c.wait_send()

    @pl.when(cross_out)
    def _():
        for c in send_a2:
            c.wait_send()


def solution(mesh):
    batch, width = mesh.shape["batch"], mesh.shape["width"]
    n = CHUNKS

    def body(teacher, student):
        rows, kt = teacher.shape
        ks = student.shape[1]
        part = rows // n
        k_all = ks + kt
        wide = 2 * rows + 2 * part * (2 * n - 1)
        dma = pltpu.SemaphoreType.DMA
        return pl.pallas_call(
            functools.partial(kernel, batch, width, rows, ks, kt, n),
            out_shape=jax.ShapeDtypeStruct((rows, ks), F32),
            in_specs=[pl.BlockSpec(memory_space=pl.ANY)] * 2,
            out_specs=pl.BlockSpec(memory_space=pltpu.VMEM),
            scratch_shapes=[
                pltpu.VMEM((2, rows, k_all), BF16),
                pltpu.VMEM((n, 2, part, k_all), BF16),
                pltpu.VMEM((n, part, k_all), BF16),
                pltpu.VMEM((width, rows // width, 2 * rows), BF16),
                pltpu.VMEM((width, rows // width, 2 * rows), BF16),
                pltpu.VMEM((n, width, part // width, wide), BF16),
                pltpu.VMEM((n, width - 1, part // width, wide), BF16),
                pltpu.VMEM((width - 1, rows // width, 2 * rows), BF16),
                pltpu.VMEM((n, width, part // width, wide), BF16),
                pltpu.VMEM((n, 2, part, ks), F32),
                pltpu.VMEM((2, rows, ks), F32),
                pltpu.VMEM((n, part, ks), F32),
                pltpu.VMEM((8, 2 * rows), F32),
                pltpu.VMEM((8, 2 * rows), F32),
                pltpu.VMEM((n, part, 128), F32),
                pltpu.VMEM((rows, 128), F32),
                pltpu.VMEM((rows, ks), BF16),
                pltpu.VMEM((2, rows, ks), BF16),
                pltpu.VMEM((rows, ks), F32),
                pltpu.VMEM((8, rows), F32),
                pltpu.VMEM((8, 2 * rows), F32),
                pltpu.VMEM((8, 2 * rows), F32),
                pltpu.VMEM((rows, ks), BF16),
                pltpu.VMEM((rows, ks), BF16),
                pltpu.VMEM((rows, ks), BF16),
                pltpu.VMEM((rows, ks), F32),
                pltpu.VMEM((8, rows), F32),
                pltpu.VMEM((8, 2 * rows), F32),
                pltpu.VMEM((8, 2 * rows), F32),
                pltpu.VMEM((8, 2 * rows), F32),
                pltpu.VMEM((1, 2 * rows), F32),
                pltpu.VMEM((n, 2, part, 128), F32),
                dma((2,)), dma((n,)), dma((n,)), dma((n,)), dma((n,)), dma((n,)), dma((n,)), dma, dma,
                dma((n + 1, width - 1)), dma((n + 1, width - 1)), dma((n + 1, width - 1)), dma((n + 1, width - 1)),
                dma((8,)), dma((8,)),
            ],
            compiler_params=pltpu.CompilerParams(
                collective_id=0, has_side_effects=True, vmem_limit_bytes=60 * 2**20
            ),
        )(teacher, student)

    specs = (P("batch", "width"), P("batch", "width"))
    return jax.shard_map(body, mesh=mesh, in_specs=specs, out_specs=P("batch", "width"), check_vma=False)
```

```python
import functools

import jax
import jax.numpy as jnp
from jax import lax
from jax.experimental import pallas as pl
from jax.experimental.pallas import tpu as pltpu
from jax.sharding import PartitionSpec as P

DT = 4096
DS = 1024
REACH = 4
MESH = pl.DeviceIdType.MESH
CHUNKS = 4
F32 = jnp.float32
BF16 = jnp.bfloat16


def dot(a, b, ca, cb):
    return lax.dot_general(a, b, (((ca,), (cb,)), ((), ())), preferred_element_type=F32)


def kernel(
    batch, width, rows, ks, kt, n,
    t_ref, s_ref, o_ref,
    bbuf, abuf, cbuf, eself, rself, esend, erecv, eselfrecv, rfull,
    acc_a, acc_b, acc_c, acc_o, sum_a, sum_b, sum_c, sum_o,
    msg_c, msg_a, msg_d, msg_x, msum_c, msum_a, msum_d, msum_x,
    got_c, got_a, got_d, got_x, gsum_c, gsum_a, gsum_d, gsum_x, msum_e, gsum_e, hb, col_k,
    in_sem, up_send, down_send, a_recv, c_recv, fwd_send, fwd_recv, b_send, b_recv,
    rs_send, rs_recv, ag_send, ag_recv, m_send, m_recv,
):
    k_all = ks + kt
    part = rows // n
    both = 2 * part
    half = both * n
    piece = part // width
    me = lax.axis_index("batch")
    wx = lax.axis_index("width")
    core = lax.rem(me, 2)
    chip = me // 2
    has_prev = chip > 0
    has_next = chip < batch // 2 - 1
    prev = (lax.rem(me + batch - 2, batch), wx)
    nxt = (lax.rem(me + 2, batch), wx)
    other = 1 - core
    mate = (me + 1 - 2 * core, wx)

    def peer(d):
        return lax.rem(wx + d, width)

    barrier = pltpu.get_barrier_semaphore()

    def greet(device):
        pl.semaphore_signal(barrier, inc=1, device_id=device, device_id_type=MESH)

    @pl.when(has_prev)
    def _():
        greet(prev)

    @pl.when(has_next)
    def _():
        greet(nxt)

    for d in range(1, width):
        greet((me, peer(d)))
    greet(mate)

    loads = []
    for q in range(n):
        span = pl.ds(q * part, part)
        loads.append(pltpu.make_async_copy(s_ref.at[span], bbuf.at[q, core, :, pl.ds(0, ks)], in_sem.at[2 * q]))
        loads.append(pltpu.make_async_copy(t_ref.at[span], bbuf.at[q, core, :, pl.ds(ks, kt)], in_sem.at[2 * q + 1]))
    for c in loads:
        c.start()

    @pl.when(jnp.logical_not(has_prev))
    def _():
        abuf[...] = jnp.zeros_like(abuf)
        gsum_c[...] = jnp.zeros_like(gsum_c)

    @pl.when(jnp.logical_not(has_next))
    def _():
        cbuf[...] = jnp.zeros_like(cbuf)
        gsum_a[...] = jnp.zeros_like(gsum_a)

    for ref in (acc_a, acc_b, acc_c, sum_a, sum_b, sum_c):
        ref[...] = jnp.zeros_like(ref)

    for c in loads:
        c.wait()

    as_int = lambda x: x.astype(jnp.int32)
    pl.semaphore_wait(barrier, width + as_int(has_prev) + as_int(has_next))

    def remote(src, dst, send, recv, device):
        return pltpu.make_async_remote_copy(
            src_ref=src, dst_ref=dst, send_sem=send, recv_sem=recv, device_id=device, device_id_type=MESH
        )

    ups = [remote(bbuf.at[q, core], abuf.at[q, core], up_send.at[q], a_recv.at[q], nxt) for q in range(n)]
    downs = [remote(bbuf.at[q, core], cbuf.at[q], down_send.at[q], c_recv.at[q], prev) for q in range(n)]
    fwds = [remote(abuf.at[q, core], abuf.at[q, core], fwd_send.at[q], fwd_recv.at[q], mate) for q in range(n)]
    shares = [remote(bbuf.at[q, core], bbuf.at[q, core], b_send.at[q], b_recv.at[q], mate) for q in range(n)]
    for q in range(n):
        @pl.when(has_next)
        def _(q=q):
            ups[q].start()

        @pl.when(has_prev)
        def _(q=q):
            downs[q].start()

        shares[q].start()

    lane = lax.broadcasted_iota(jnp.int32, (1, k_all), 1)
    signs = jnp.where(lane < ks, -float(DT // DS), 1.0).astype(F32)
    signs_low = signs.astype(BF16)

    def half_norm(x):
        wide = x.astype(F32)
        return 0.5 * jnp.sum(wide * wide * signs, axis=1, keepdims=True)

    def as_row(col):
        m = col.shape[0]
        pieces = [
            jnp.transpose(jnp.broadcast_to(col[i : i + 128, 0:1], (128, 128)))[0:1, :] for i in range(0, m, 128)
        ]
        return pieces[0] if len(pieces) == 1 else jnp.concatenate(pieces, axis=1)

    def as_col(row):
        m = row.shape[1]
        pieces = [jnp.transpose(jnp.broadcast_to(row[0:1, i : i + 128], (128, 128))) for i in range(0, m, 128)]
        return pieces[0] if len(pieces) == 1 else jnp.concatenate(pieces, axis=0)

    def join(parts, axis):
        return parts[0] if len(parts) == 1 else jnp.concatenate(parts, axis=axis)

    scale = 2.0 / DT

    def scatter(i, src, dst):
        cs = [
            remote(src.at[peer(d)], dst.at[d - 1], rs_send.at[i, d - 1], rs_recv.at[i, d - 1], (me, peer(d)))
            for d in range(1, width)
        ]
        for c in cs:
            c.start()
        return cs

    def reduce(cs, src, dst, mask):
        total = src[wx].astype(F32)
        for c in cs:
            c.wait_recv()
        for d in range(width - 1):
            total = total + dst[d].astype(F32)
        if mask is not None:
            total = jnp.where(mask, total, 0.0)
        return total.astype(BF16)

    def gather(stage, out, low):
        out[wx] = low
        cs = [
            remote(out.at[wx], out.at[wx], ag_send.at[stage, d - 1], ag_recv.at[stage, d - 1], (me, peer(d)))
            for d in range(1, width)
        ]
        for c in cs:
            c.start()
        return cs

    scatters = [None] * (n + 1)
    gathers = [None] * (n + 1)

    half_o = []
    for q in range(n):
        shares[q].wait_recv()
        hb[:, q * both : (q + 1) * both] = as_row(half_norm(bbuf[q].reshape(both, k_all)))
        half_o.append(half_norm(bbuf[q, core]))
    mid, span = rows // 2, n // 2

    def half_block(ref, i, k, wide):
        return ref[pl.ds(i * span, span), k, :, 0:wide].reshape(mid, wide)

    match = [lax.rem(i + core, 2) for i in range(2)]

    def half_blocks(wide):
        own_halves = [half_block(bbuf, i, core, wide) for i in range(2)]
        return own_halves, [half_block(bbuf, match[i], other, wide) for i in range(2)]

    mine, theirs = half_blocks(k_all)
    norm_m = [half_norm(x) for x in mine]
    row_m = [as_row(x) for x in norm_m]
    row_t = [as_row(half_norm(x)) for x in theirs]
    pairs = [(0, mine[0], row_m[0]), (1, mine[0], row_m[0]), (1, mine[1], row_m[1])]
    pairs += [(0, theirs[0], row_t[0]), (1, theirs[1], row_t[1])]
    for i, (left, right, row) in enumerate(pairs):
        e = (dot(mine[left] * signs_low, right, 1, 1) - norm_m[left] - row) * scale
        eself[:, :, i * mid : (i + 1) * mid] = e.astype(BF16).reshape(width, mid // width, mid)
    scatters[0] = scatter(0, eself, eselfrecv)

    def view(ref, q, at, wide):
        return ref.at[q, :, :, pl.ds(at, wide)]

    def finish(stage):
        if stage == 0:
            gathers[0] = gather(0, rself, reduce(scatters[0], eself, eselfrecv, None))
            return
        q = stage - 1
        lanes = lax.broadcasted_iota(jnp.int32, (1, 2 * half), 1)
        with_b = lanes < both * (n - q)
        b_with_a = lanes >= half + both * (q + 1)
        far = jnp.logical_and(lax.rem(lanes // part, 2) == 0, core == 1)
        c_with_a = jnp.logical_and(jnp.logical_and(has_prev, has_next), jnp.logical_not(far))
        mask = jnp.where(
            with_b, as_int(has_next), jnp.where(b_with_a, as_int(has_prev), as_int(c_with_a))
        )
        gathers[stage] = gather(stage, rfull.at[q], reduce(scatters[stage], esend.at[q], erecv.at[q], mask > 0))

    def row_sum(r):
        return jnp.broadcast_to(jnp.sum(r.astype(F32), axis=1, keepdims=True), (r.shape[0], 128))

    def col_sum(r):
        return jnp.sum(r.astype(F32), axis=0, keepdims=True)

    def pull(stage):
        for c in gathers[stage]:
            c.wait_recv()
        if stage == 0:
            r = rself[...].reshape(mid, 5 * mid)
            r00, r10, r11, x0, x1 = [r[:, i * mid : (i + 1) * mid] for i in range(5)]
            (s0, s1), (t0, t1) = half_blocks(ks)
            acc_o[0:span] = (dot(r00, s0, 1, 0) + dot(r10, s1, 0, 0) + dot(x0, t0, 1, 0)).reshape(span, part, ks)
            acc_o[span:n] = (dot(r10, s0, 1, 0) + dot(r11, s1, 1, 0) + dot(x1, t1, 1, 0)).reshape(span, part, ks)
            sum_o[0:span] = (row_sum(r00) + row_sum(x0) + as_col(col_sum(r10))).reshape(span, part, 128)
            sum_o[span:n] = (row_sum(r10) + row_sum(r11) + row_sum(x1)).reshape(span, part, 128)
            for i, (x, s_i) in enumerate([(x0, s0), (x1, s1)]):
                at = pl.ds(match[i] * span, span)
                acc_b[at, other] += dot(x, s_i, 0, 0).reshape(span, part, ks)
                msum_e[match[i]] = jnp.broadcast_to(col_sum(x), (8, mid))
            return
        q = stage - 1
        last = stage == n
        b_end = both * (n - q)
        r = rfull[q].reshape(part, 2 * half)
        rb, ra = r[:, 0:b_end], r[:, b_end:half]
        rs = join([r[:, half + both * i : half + both * (i + 1)] for i in range(n)], 0)
        sc = cbuf[q, :, 0:ks]
        sa = abuf[q, :, :, 0:ks].reshape(both, ks)
        left = [sc] + [cbuf[p, :, 0:ks] for p in range(q)] + [bbuf[p, core, :, 0:ks] for p in range(q + 1, n)]
        acc_a[q] += dot(rs, join(left, 0), 0, 0).reshape(2, part, ks)
        sum_a[0:1, both * q : both * (q + 1)] += col_sum(rs)
        if q:
            acc_a[0:q] += dot(ra, sc, 0, 0).reshape(q, 2, part, ks)
            sum_a[0:1, 0 : both * q] += col_sum(ra)
        if last:
            send_rows_a()
        x = dot(rs, sa, 1, 0)
        xs = row_sum(rs)
        y = dot(rb, bbuf[q:n, :, :, 0:ks].reshape(b_end, ks), 1, 0)
        if q:
            y += dot(ra, abuf[0:q, :, :, 0:ks].reshape(both * q, ks), 1, 0)
        acc_c[q] += x[0:part] + y
        sum_c[q] += xs[0:part] + row_sum(r[:, 0:half])
        if q:
            acc_c[0:q] += x[part : part * (q + 1)].reshape(q, part, ks)
            sum_c[0:q] += xs[part : part * (q + 1)].reshape(q, part, 128)
        if last:
            send_rows_c()
        acc_b[q:n] += dot(rb, sc, 0, 0).reshape(n - q, 2, part, ks)
        sum_b[0:1, both * q : half] += col_sum(rb)
        if last:
            send_rows_d()
        else:
            acc_o[q + 1 : n] += x[part * (q + 1) :].reshape(n - 1 - q, part, ks)
            sum_o[q + 1 : n] += xs[part * (q + 1) :].reshape(n - 1 - q, part, 128)

    def pair(i, src, dst, ssrc, sdst, device):
        return [
            remote(src, dst, m_send.at[2 * i], m_recv.at[2 * i], device),
            remote(ssrc, sdst, m_send.at[2 * i + 1], m_recv.at[2 * i + 1], device),
        ]

    send_c = pair(0, msg_c, got_c, msum_c, gsum_c, nxt)
    send_a = pair(1, msg_a, got_a, msum_a, gsum_a, prev)
    send_x = pair(2, msg_x, got_x, msum_x, gsum_x, mate)
    send_d = pair(3, msg_d, got_d, msum_d, gsum_d, mate)
    send_d.append(remote(msum_e, gsum_e, m_send.at[8], m_recv.at[8], mate))

    def begin(cs):
        for c in cs:
            c.start()

    def arrive(cs):
        for c in cs:
            c.wait_recv()

    def send_rows_a():
        @pl.when(has_prev)
        def _():
            msg_x[...] = acc_a[:, other].reshape(rows, ks)
            msum_x[...] = jnp.broadcast_to(sum_a[0:1], (8, half))
            begin(send_x)

    def send_rows_c():
        @pl.when(has_next)
        def _():
            msg_c[...] = acc_c[...].reshape(rows, ks).astype(BF16)
            msum_c[...] = jnp.broadcast_to(as_row(sum_c[...].reshape(rows, 128)), (8, rows))
            begin(send_c)

        @pl.when(has_prev)
        def _():
            arrive(send_x)
            msg_a[...] = (acc_a[:, core].reshape(rows, ks) + got_x[...]).astype(BF16)
            msum_a[...] = jnp.broadcast_to(sum_a[0:1] + gsum_x[0:1], (8, half))
            begin(send_a)

    def send_rows_d():
        msg_d[...] = acc_b[:, other].reshape(rows, ks)
        msum_d[...] = jnp.broadcast_to(sum_b[0:1], (8, half))
        begin(send_d)

    half_c, half_a = [], []
    for q in range(n):
        stage = 1 + q

        @pl.when(has_prev)
        def _(q=q):
            ups[q].wait_recv()
            fwds[q].start()

        @pl.when(has_next)
        def _(q=q):
            downs[q].wait_recv()

        half_c.append(half_norm(cbuf[q]))

        def put(at, tile):
            wide = tile.shape[1]
            esend[q, :, :, at : at + wide] = (tile * scale).astype(BF16).reshape(width, piece, wide)

        c_scaled = cbuf[q] * signs_low
        b_end = both * (n - q)
        put(0, dot(c_scaled, bbuf[q:n].reshape(b_end, k_all), 1, 1) - half_c[q] - hb[:, both * q : half])
        if q:
            g = dot(c_scaled, abuf[0:q].reshape(both * q, k_all), 1, 1)
            put(b_end, g - half_c[q] - join(half_a, 1))
        scatters[stage] = scatter(2 * q + 1, view(esend, q, 0, half), view(erecv, q, 0, half))

        @pl.when(has_prev)
        def _(q=q):
            fwds[q].wait_recv()

        a_q = abuf[q].reshape(both, k_all)
        half_a.append(as_row(half_norm(a_q)))
        left = [cbuf[q]] + [cbuf[p] for p in range(q)] + [bbuf[p, core] for p in range(q + 1, n)]
        norms = [half_c[q]] + half_c[0:q] + half_o[q + 1 : n]
        g = dot(join(left, 0) * signs_low, a_q, 1, 1)
        for i in range(n):
            put(half + both * i, g[part * i : part * (i + 1)] - norms[i] - half_a[q])
        scatters[stage] += scatter(2 * q + 2, view(esend, q, half, half), view(erecv, q, half, half))
        finish(stage - 1)
        if q:
            pull(stage - 2)
    finish(n)
    pull(n - 1)
    pull(n)

    o_ref[...] = acc_b[:, core].reshape(rows, ks) + acc_o[...].reshape(rows, ks)
    arrive(send_d)
    o_ref[...] += got_d[...]

    @pl.when(has_prev)
    def _():
        arrive(send_c)
        o_ref[...] += got_c[...].astype(F32)

    @pl.when(has_next)
    def _():
        arrive(send_a)
        o_ref[...] += got_a[...].astype(F32)

    col_k[...] = as_col(gsum_a[0:1] + gsum_d[0:1] + sum_b[0:1]).reshape(n, 2, part, 128)
    total = as_col(gsum_c[0:1]) + col_k[:, core].reshape(rows, 128) + sum_o[...].reshape(rows, 128)
    total += join([as_col(gsum_e[i, 0:1]) for i in range(2)], 0)
    near = (2 * REACH + 1) * rows
    s_own = bbuf[:, core, :, 0:ks].reshape(rows, ks).astype(F32)
    for i in range(0, ks, 128):
        o_ref[:, i : i + 128] = (s_own[:, i : i + 128] * total - o_ref[:, i : i + 128]) * (1.0 / near)

    for cs in [shares, send_d] + scatters + gathers:
        for c in cs:
            c.wait_send()

    @pl.when(has_next)
    def _():
        for c in ups + send_c:
            c.wait_send()

    @pl.when(has_prev)
    def _():
        for c in downs + fwds + send_a + send_x:
            c.wait_send()


def solution(mesh):
    batch, width = mesh.shape["batch"], mesh.shape["width"]
    n = CHUNKS

    def body(teacher, student):
        rows, kt = teacher.shape
        ks = student.shape[1]
        part = rows // n
        k_all = ks + kt
        half = 2 * rows
        wide = 2 * half
        dma = pltpu.SemaphoreType.DMA
        low = lambda *shape: pltpu.VMEM(shape, BF16)
        full = lambda *shape: pltpu.VMEM(shape, F32)
        return pl.pallas_call(
            functools.partial(kernel, batch, width, rows, ks, kt, n),
            out_shape=jax.ShapeDtypeStruct((rows, ks), F32),
            in_specs=[pl.BlockSpec(memory_space=pl.ANY)] * 2,
            out_specs=pl.BlockSpec(memory_space=pltpu.VMEM),
            scratch_shapes=[
                low(n, 2, part, k_all), low(n, 2, part, k_all), low(n, part, k_all),
                low(width, rows // 2 // width, 5 * rows // 2), low(width, rows // 2 // width, 5 * rows // 2),
                low(n, width, part // width, wide), low(n, width - 1, part // width, wide),
                low(width - 1, rows // 2 // width, 5 * rows // 2), low(n, width, part // width, wide),
                full(n, 2, part, ks), full(n, 2, part, ks), full(n, part, ks), full(n, part, ks),
                full(8, half), full(8, half), full(n, part, 128), full(n, part, 128),
                low(rows, ks), low(rows, ks), full(rows, ks), full(rows, ks),
                full(8, rows), full(8, half), full(8, half), full(8, half),
                low(rows, ks), low(rows, ks), full(rows, ks), full(rows, ks),
                full(8, rows), full(8, half), full(8, half), full(8, half),
                full(2, 8, rows // 2), full(2, 8, rows // 2), full(1, half), full(n, 2, part, 128),
                dma((2 * n,)), dma((n,)), dma((n,)), dma((n,)), dma((n,)), dma((n,)), dma((n,)), dma((n,)), dma((n,)),
                dma((2 * n + 1, width - 1)), dma((2 * n + 1, width - 1)),
                dma((n + 1, width - 1)), dma((n + 1, width - 1)),
                dma((9,)), dma((9,)),
            ],
            compiler_params=pltpu.CompilerParams(
                collective_id=0, has_side_effects=True, vmem_limit_bytes=60 * 2**20
            ),
        )(teacher, student)

    specs = (P("batch", "width"), P("batch", "width"))
    return jax.shard_map(body, mesh=mesh, in_specs=specs, out_specs=P("batch", "width"), check_vma=False)
```

```python
import functools

import jax
import jax.numpy as jnp
from jax import lax
from jax.experimental import pallas as pl
from jax.experimental.pallas import tpu as pltpu
from jax.sharding import PartitionSpec as P

DT = 4096
DS = 1024
REACH = 4
MESH = pl.DeviceIdType.MESH
CHUNKS = 4
F32 = jnp.float32
BF16 = jnp.bfloat16


def dot(a, b, ca, cb):
    return lax.dot_general(a, b, (((ca,), (cb,)), ((), ())), preferred_element_type=F32)


def kernel(
    batch, width, rows, ks, kt, n,
    t_ref, s_ref, o_ref,
    bbuf, abuf, cbuf, eself, rself, esend, erecv, eselfrecv, rfull,
    acc_a, acc_b, acc_c, acc_o, sum_a, sum_b, sum_c, sum_o,
    msg_c, msg_a, msg_d, msg_x, msum_c, msum_a, msum_d, msum_x,
    got_c, got_a, got_d, got_x, gsum_c, gsum_a, gsum_d, gsum_x, msum_e, gsum_e, hb, col_k,
    in_sem, up_send, down_send, a_recv, c_recv, fwd_send, fwd_recv, b_send, b_recv,
    rs_send, rs_recv, ag_send, ag_recv, m_send, m_recv,
):
    k_all = ks + kt
    part = rows // n
    both = 2 * part
    half = both * n
    piece = part // width
    me = lax.axis_index("batch")
    wx = lax.axis_index("width")
    core = lax.rem(me, 2)
    chip = me // 2
    has_prev = chip > 0
    has_next = chip < batch // 2 - 1
    prev = (lax.rem(me + batch - 2, batch), wx)
    nxt = (lax.rem(me + 2, batch), wx)
    other = 1 - core
    mate = (me + 1 - 2 * core, wx)

    def peer(d):
        return lax.rem(wx + d, width)

    barrier = pltpu.get_barrier_semaphore()

    def greet(device):
        pl.semaphore_signal(barrier, inc=1, device_id=device, device_id_type=MESH)

    @pl.when(has_prev)
    def _():
        greet(prev)

    @pl.when(has_next)
    def _():
        greet(nxt)

    for d in range(1, width):
        greet((me, peer(d)))
    greet(mate)

    loads = []
    for q in range(n):
        span = pl.ds(q * part, part)
        loads.append(pltpu.make_async_copy(s_ref.at[span], bbuf.at[q, core, :, pl.ds(0, ks)], in_sem.at[2 * q]))
        loads.append(pltpu.make_async_copy(t_ref.at[span], bbuf.at[q, core, :, pl.ds(ks, kt)], in_sem.at[2 * q + 1]))
    for c in loads:
        c.start()

    @pl.when(jnp.logical_not(has_prev))
    def _():
        abuf[...] = jnp.zeros_like(abuf)
        gsum_c[...] = jnp.zeros_like(gsum_c)

    @pl.when(jnp.logical_not(has_next))
    def _():
        cbuf[...] = jnp.zeros_like(cbuf)
        gsum_a[...] = jnp.zeros_like(gsum_a)

    for ref in (acc_a, acc_b, acc_c, sum_a, sum_b, sum_c):
        ref[...] = jnp.zeros_like(ref)

    for c in loads:
        c.wait()

    as_int = lambda x: x.astype(jnp.int32)
    pl.semaphore_wait(barrier, width + as_int(has_prev) + as_int(has_next))

    def remote(src, dst, send, recv, device):
        return pltpu.make_async_remote_copy(
            src_ref=src, dst_ref=dst, send_sem=send, recv_sem=recv, device_id=device, device_id_type=MESH
        )

    ups = [remote(bbuf.at[q, core], abuf.at[q, core], up_send.at[q], a_recv.at[q], nxt) for q in range(n)]
    downs = [remote(bbuf.at[q, core], cbuf.at[q], down_send.at[q], c_recv.at[q], prev) for q in range(n)]
    fwds = [remote(abuf.at[q, core], abuf.at[q, core], fwd_send.at[q], fwd_recv.at[q], mate) for q in range(n)]
    shares = [remote(bbuf.at[q, core], bbuf.at[q, core], b_send.at[q], b_recv.at[q], mate) for q in range(n)]
    for c in shares:
        c.start()
    for q in range(n):
        @pl.when(has_next)
        def _(q=q):
            ups[q].start()

        @pl.when(has_prev)
        def _(q=q):
            downs[q].start()

    lane = lax.broadcasted_iota(jnp.int32, (1, k_all), 1)
    signs = jnp.where(lane < ks, -float(DT // DS), 1.0).astype(F32)
    signs_low = signs.astype(BF16)

    def half_norm(x):
        wide = x.astype(F32)
        return 0.5 * jnp.sum(wide * wide * signs, axis=1, keepdims=True)

    def as_row(col):
        m = col.shape[0]
        pieces = [
            jnp.transpose(jnp.broadcast_to(col[i : i + 128, 0:1], (128, 128)))[0:1, :] for i in range(0, m, 128)
        ]
        return pieces[0] if len(pieces) == 1 else jnp.concatenate(pieces, axis=1)

    def as_col(row):
        m = row.shape[1]
        pieces = [jnp.transpose(jnp.broadcast_to(row[0:1, i : i + 128], (128, 128))) for i in range(0, m, 128)]
        return pieces[0] if len(pieces) == 1 else jnp.concatenate(pieces, axis=0)

    def join(parts, axis):
        return parts[0] if len(parts) == 1 else jnp.concatenate(parts, axis=axis)

    scale = 2.0 / DT

    far_first = sorted(range(width - 1), key=lambda i: -min(i + 1, width - 1 - i))

    def scatter(i, src, dst):
        cs = [
            remote(src.at[peer(d)], dst.at[d - 1], rs_send.at[i, d - 1], rs_recv.at[i, d - 1], (me, peer(d)))
            for d in range(1, width)
        ]
        for i in far_first:
            cs[i].start()
        return cs

    def reduce(cs, src, dst, mask):
        total = src[wx].astype(F32)
        for c in cs:
            c.wait_recv()
        for d in range(width - 1):
            total = total + dst[d].astype(F32)
        if mask is not None:
            total = jnp.where(mask, total, 0.0)
        return total.astype(BF16)

    def gather(stage, out, low):
        out[wx] = low
        cs = [
            remote(out.at[wx], out.at[wx], ag_send.at[stage, d - 1], ag_recv.at[stage, d - 1], (me, peer(d)))
            for d in range(1, width)
        ]
        for i in far_first:
            cs[i].start()
        return cs

    scatters = [None] * (n + 1)
    gathers = [None] * (n + 1)

    half_o = []
    for q in range(n):
        shares[q].wait_recv()
        hb[:, q * both : (q + 1) * both] = as_row(half_norm(bbuf[q].reshape(both, k_all)))
        half_o.append(half_norm(bbuf[q, core]))
    mid, span = rows // 2, n // 2

    def half_block(ref, i, k, wide):
        return ref[pl.ds(i * span, span), k, :, 0:wide].reshape(mid, wide)

    match = [lax.rem(i + core, 2) for i in range(2)]

    def half_blocks(wide):
        own_halves = [half_block(bbuf, i, core, wide) for i in range(2)]
        return own_halves, [half_block(bbuf, match[i], other, wide) for i in range(2)]

    mine, theirs = half_blocks(k_all)
    norm_m = [half_norm(x) for x in mine]
    row_m = [as_row(x) for x in norm_m]
    row_t = [as_row(half_norm(x)) for x in theirs]
    pairs = [(0, mine[0], row_m[0]), (1, mine[0], row_m[0]), (1, mine[1], row_m[1])]
    pairs += [(0, theirs[0], row_t[0]), (1, theirs[1], row_t[1])]
    for i, (left, right, row) in enumerate(pairs):
        e = (dot(mine[left] * signs_low, right, 1, 1) - norm_m[left] - row) * scale
        eself[:, :, i * mid : (i + 1) * mid] = e.astype(BF16).reshape(width, mid // width, mid)
    scatters[0] = scatter(0, eself, eselfrecv)

    def view(ref, q, at, wide):
        return ref.at[q, :, :, pl.ds(at, wide)]

    def finish(stage):
        if stage == 0:
            gathers[0] = gather(0, rself, reduce(scatters[0], eself, eselfrecv, None))
            return
        q = stage - 1
        lanes = lax.broadcasted_iota(jnp.int32, (1, 2 * half), 1)
        with_b = lanes < both * (n - q)
        b_with_a = lanes >= half + both * (q + 1)
        far = jnp.logical_and(lax.rem(lanes // part, 2) == 0, core == 1)
        c_with_a = jnp.logical_and(jnp.logical_and(has_prev, has_next), jnp.logical_not(far))
        mask = jnp.where(
            with_b, as_int(has_next), jnp.where(b_with_a, as_int(has_prev), as_int(c_with_a))
        )
        gathers[stage] = []
        for h in range(2):
            cs = scatters[stage][h * (width - 1) : (h + 1) * (width - 1)]
            send, recv, out = [view(ref, q, h * half, half) for ref in (esend, erecv, rfull)]
            low = reduce(cs, send, recv, mask[:, h * half : (h + 1) * half] > 0)
            gathers[stage] += gather(1 + 2 * q + h, out, low)

    def row_sum(r):
        return jnp.broadcast_to(jnp.sum(r.astype(F32), axis=1, keepdims=True), (r.shape[0], 128))

    def col_sum(r):
        return jnp.sum(r.astype(F32), axis=0, keepdims=True)

    def pull(stage):
        for c in gathers[stage]:
            c.wait_recv()
        if stage == 0:
            r = rself[...].reshape(mid, 5 * mid)
            r00, r10, r11, x0, x1 = [r[:, i * mid : (i + 1) * mid] for i in range(5)]
            (s0, s1), (t0, t1) = half_blocks(ks)
            acc_o[0:span] = (dot(r00, s0, 1, 0) + dot(r10, s1, 0, 0) + dot(x0, t0, 1, 0)).reshape(span, part, ks)
            acc_o[span:n] = (dot(r10, s0, 1, 0) + dot(r11, s1, 1, 0) + dot(x1, t1, 1, 0)).reshape(span, part, ks)
            sum_o[0:span] = (row_sum(r00) + row_sum(x0) + as_col(col_sum(r10))).reshape(span, part, 128)
            sum_o[span:n] = (row_sum(r10) + row_sum(r11) + row_sum(x1)).reshape(span, part, 128)
            for i, (x, s_i) in enumerate([(x0, s0), (x1, s1)]):
                at = pl.ds(match[i] * span, span)
                acc_b[at, other] += dot(x, s_i, 0, 0).reshape(span, part, ks)
                msum_e[match[i]] = jnp.broadcast_to(col_sum(x), (8, mid))
            return
        q = stage - 1
        last = stage == n
        b_end = both * (n - q)
        r = rfull[q].reshape(part, 2 * half)
        rb, ra = r[:, 0:b_end], r[:, b_end:half]
        rs = join([r[:, half + both * i : half + both * (i + 1)] for i in range(n)], 0)
        sc = cbuf[q, :, 0:ks]
        sa = abuf[q, :, :, 0:ks].reshape(both, ks)
        left = [sc] + [cbuf[p, :, 0:ks] for p in range(q)] + [bbuf[p, core, :, 0:ks] for p in range(q + 1, n)]
        acc_a[q] += dot(rs, join(left, 0), 0, 0).reshape(2, part, ks)
        sum_a[0:1, both * q : both * (q + 1)] += col_sum(rs)
        if q:
            acc_a[0:q] += dot(ra, sc, 0, 0).reshape(q, 2, part, ks)
            sum_a[0:1, 0 : both * q] += col_sum(ra)
        if last:
            send_rows_a()
        x = dot(rs, sa, 1, 0)
        xs = row_sum(rs)
        y = dot(rb, bbuf[q:n, :, :, 0:ks].reshape(b_end, ks), 1, 0)
        if q:
            y += dot(ra, abuf[0:q, :, :, 0:ks].reshape(both * q, ks), 1, 0)
        acc_c[q] += x[0:part] + y
        sum_c[q] += xs[0:part] + row_sum(r[:, 0:half])
        if q:
            acc_c[0:q] += x[part : part * (q + 1)].reshape(q, part, ks)
            sum_c[0:q] += xs[part : part * (q + 1)].reshape(q, part, 128)
        if last:
            send_rows_c()
        acc_b[q:n] += dot(rb, sc, 0, 0).reshape(n - q, 2, part, ks)
        sum_b[0:1, both * q : half] += col_sum(rb)
        if last:
            send_rows_d()
        else:
            acc_o[q + 1 : n] += x[part * (q + 1) :].reshape(n - 1 - q, part, ks)
            sum_o[q + 1 : n] += xs[part * (q + 1) :].reshape(n - 1 - q, part, 128)

    def pair(i, src, dst, ssrc, sdst, device):
        return [
            remote(src, dst, m_send.at[2 * i], m_recv.at[2 * i], device),
            remote(ssrc, sdst, m_send.at[2 * i + 1], m_recv.at[2 * i + 1], device),
        ]

    send_c = pair(0, msg_c, got_c, msum_c, gsum_c, nxt)
    send_a = pair(1, msg_a, got_a, msum_a, gsum_a, prev)
    send_x = pair(2, msg_x, got_x, msum_x, gsum_x, mate)
    send_d = pair(3, msg_d, got_d, msum_d, gsum_d, mate)
    send_d.append(remote(msum_e, gsum_e, m_send.at[8], m_recv.at[8], mate))

    def begin(cs):
        for c in cs:
            c.start()

    def arrive(cs):
        for c in cs:
            c.wait_recv()

    def send_rows_a():
        @pl.when(has_prev)
        def _():
            msg_x[...] = acc_a[:, other].reshape(rows, ks)
            msum_x[...] = jnp.broadcast_to(sum_a[0:1], (8, half))
            begin(send_x)

    def send_rows_c():
        @pl.when(has_next)
        def _():
            msg_c[...] = acc_c[...].reshape(rows, ks).astype(BF16)
            msum_c[...] = jnp.broadcast_to(as_row(sum_c[...].reshape(rows, 128)), (8, rows))
            begin(send_c)

        @pl.when(has_prev)
        def _():
            arrive(send_x)
            msg_a[...] = (acc_a[:, core].reshape(rows, ks) + got_x[...]).astype(BF16)
            msum_a[...] = jnp.broadcast_to(sum_a[0:1] + gsum_x[0:1], (8, half))
            begin(send_a)

    def send_rows_d():
        msg_d[...] = acc_b[:, other].reshape(rows, ks)
        msum_d[...] = jnp.broadcast_to(sum_b[0:1], (8, half))
        begin(send_d)

    half_c, half_a = [], []
    for q in range(n):
        stage = 1 + q

        @pl.when(has_prev)
        def _(q=q):
            ups[q].wait_recv()
            fwds[q].start()

        @pl.when(has_next)
        def _(q=q):
            downs[q].wait_recv()

        half_c.append(half_norm(cbuf[q]))

        def put(at, tile):
            wide = tile.shape[1]
            esend[q, :, :, at : at + wide] = (tile * scale).astype(BF16).reshape(width, piece, wide)

        c_scaled = cbuf[q] * signs_low
        b_end = both * (n - q)
        put(0, dot(c_scaled, bbuf[q:n].reshape(b_end, k_all), 1, 1) - half_c[q] - hb[:, both * q : half])
        if q:
            g = dot(c_scaled, abuf[0:q].reshape(both * q, k_all), 1, 1)
            put(b_end, g - half_c[q] - join(half_a, 1))
        scatters[stage] = scatter(2 * q + 1, view(esend, q, 0, half), view(erecv, q, 0, half))

        @pl.when(has_prev)
        def _(q=q):
            fwds[q].wait_recv()

        a_q = abuf[q].reshape(both, k_all)
        half_a.append(as_row(half_norm(a_q)))
        left = [cbuf[q]] + [cbuf[p] for p in range(q)] + [bbuf[p, core] for p in range(q + 1, n)]
        norms = [half_c[q]] + half_c[0:q] + half_o[q + 1 : n]
        g = dot(join(left, 0) * signs_low, a_q, 1, 1)
        for i in range(n):
            put(half + both * i, g[part * i : part * (i + 1)] - norms[i] - half_a[q])
        scatters[stage] += scatter(2 * q + 2, view(esend, q, half, half), view(erecv, q, half, half))
        finish(stage - 1)
        if q > 1:
            pull(stage - 3)
    pull(n - 2)
    finish(n)
    pull(n - 1)
    pull(n)

    o_ref[...] = acc_b[:, core].reshape(rows, ks) + acc_o[...].reshape(rows, ks)
    arrive(send_d)
    o_ref[...] += got_d[...]

    @pl.when(has_prev)
    def _():
        arrive(send_c)
        o_ref[...] += got_c[...].astype(F32)

    @pl.when(has_next)
    def _():
        arrive(send_a)
        o_ref[...] += got_a[...].astype(F32)

    col_k[...] = as_col(gsum_a[0:1] + gsum_d[0:1] + sum_b[0:1]).reshape(n, 2, part, 128)
    total = as_col(gsum_c[0:1]) + col_k[:, core].reshape(rows, 128) + sum_o[...].reshape(rows, 128)
    total += join([as_col(gsum_e[i, 0:1]) for i in range(2)], 0)
    near = (2 * REACH + 1) * rows
    s_own = bbuf[:, core, :, 0:ks].reshape(rows, ks).astype(F32)
    for i in range(0, ks, 128):
        o_ref[:, i : i + 128] = (s_own[:, i : i + 128] * total - o_ref[:, i : i + 128]) * (1.0 / near)

    for cs in [shares, send_d] + scatters + gathers:
        for c in cs:
            c.wait_send()

    @pl.when(has_next)
    def _():
        for c in ups + send_c:
            c.wait_send()

    @pl.when(has_prev)
    def _():
        for c in downs + fwds + send_a + send_x:
            c.wait_send()


def solution(mesh):
    batch, width = mesh.shape["batch"], mesh.shape["width"]
    n = CHUNKS

    def body(teacher, student):
        rows, kt = teacher.shape
        ks = student.shape[1]
        part = rows // n
        k_all = ks + kt
        half = 2 * rows
        wide = 2 * half
        dma = pltpu.SemaphoreType.DMA
        low = lambda *shape: pltpu.VMEM(shape, BF16)
        full = lambda *shape: pltpu.VMEM(shape, F32)
        return pl.pallas_call(
            functools.partial(kernel, batch, width, rows, ks, kt, n),
            out_shape=jax.ShapeDtypeStruct((rows, ks), F32),
            in_specs=[pl.BlockSpec(memory_space=pl.ANY)] * 2,
            out_specs=pl.BlockSpec(memory_space=pltpu.VMEM),
            scratch_shapes=[
                low(n, 2, part, k_all), low(n, 2, part, k_all), low(n, part, k_all),
                low(width, rows // 2 // width, 5 * rows // 2), low(width, rows // 2 // width, 5 * rows // 2),
                low(n, width, part // width, wide), low(n, width - 1, part // width, wide),
                low(width - 1, rows // 2 // width, 5 * rows // 2), low(n, width, part // width, wide),
                full(n, 2, part, ks), full(n, 2, part, ks), full(n, part, ks), full(n, part, ks),
                full(8, half), full(8, half), full(n, part, 128), full(n, part, 128),
                low(rows, ks), low(rows, ks), full(rows, ks), full(rows, ks),
                full(8, rows), full(8, half), full(8, half), full(8, half),
                low(rows, ks), low(rows, ks), full(rows, ks), full(rows, ks),
                full(8, rows), full(8, half), full(8, half), full(8, half),
                full(2, 8, rows // 2), full(2, 8, rows // 2), full(1, half), full(n, 2, part, 128),
                dma((2 * n,)), dma((n,)), dma((n,)), dma((n,)), dma((n,)), dma((n,)), dma((n,)), dma((n,)), dma((n,)),
                dma((2 * n + 1, width - 1)), dma((2 * n + 1, width - 1)),
                dma((2 * n + 1, width - 1)), dma((2 * n + 1, width - 1)),
                dma((9,)), dma((9,)),
            ],
            compiler_params=pltpu.CompilerParams(
                collective_id=0, has_side_effects=True, vmem_limit_bytes=60 * 2**20
            ),
        )(teacher, student)

    specs = (P("batch", "width"), P("batch", "width"))
    return jax.shard_map(body, mesh=mesh, in_specs=specs, out_specs=P("batch", "width"), check_vma=False)
```

```python
import functools

import jax
import jax.numpy as jnp
from jax import lax
from jax.experimental import pallas as pl
from jax.experimental.pallas import tpu as pltpu
from jax.sharding import PartitionSpec as P

DT = 4096
DS = 1024
REACH = 4
MESH = pl.DeviceIdType.MESH
CHUNKS = 4
F32 = jnp.float32
BF16 = jnp.bfloat16


def dot(a, b, ca, cb):
    return lax.dot_general(a, b, (((ca,), (cb,)), ((), ())), preferred_element_type=F32)


def kernel(
    batch, width, rows, ks, kt, n,
    t_ref, s_ref, o_ref,
    bbuf, abuf, cbuf, eself, rself, esend, erecv, eselfrecv, rfull,
    acc_a, acc_b, acc_c, acc_o, sum_a, sum_b, sum_c, sum_o,
    msg_c, msg_a, msg_d, msg_x, msum_c, msum_a, msum_d, msum_x,
    got_c, got_a, got_d, got_x, gsum_c, gsum_a, gsum_d, gsum_x, msum_e, gsum_e, hb, col_k,
    in_sem, up_send, down_send, a_recv, c_recv, fwd_send, fwd_recv, b_send, b_recv,
    rs_send, rs_recv, ag_send, ag_recv, m_send, m_recv,
):
    k_all = ks + kt
    part = rows // n
    both = 2 * part
    half = both * n
    piece = part // width
    me = lax.axis_index("batch")
    wx = lax.axis_index("width")
    core = lax.rem(me, 2)
    chip = me // 2
    has_prev = chip > 0
    has_next = chip < batch // 2 - 1
    prev = (lax.rem(me + batch - 2, batch), wx)
    nxt = (lax.rem(me + 2, batch), wx)
    other = 1 - core
    mate = (me + 1 - 2 * core, wx)

    def peer(d):
        return lax.rem(wx + d, width)

    barrier = pltpu.get_barrier_semaphore()

    def greet(device):
        pl.semaphore_signal(barrier, inc=1, device_id=device, device_id_type=MESH)

    @pl.when(has_prev)
    def _():
        greet(prev)

    @pl.when(has_next)
    def _():
        greet(nxt)

    for d in range(1, width):
        greet((me, peer(d)))
    greet(mate)

    loads = []
    for q in range(n):
        span = pl.ds(q * part, part)
        loads.append(pltpu.make_async_copy(s_ref.at[span], bbuf.at[q, core, :, pl.ds(0, ks)], in_sem.at[2 * q]))
        loads.append(pltpu.make_async_copy(t_ref.at[span], bbuf.at[q, core, :, pl.ds(ks, kt)], in_sem.at[2 * q + 1]))
    for c in loads:
        c.start()

    @pl.when(jnp.logical_not(has_prev))
    def _():
        abuf[...] = jnp.zeros_like(abuf)
        gsum_c[...] = jnp.zeros_like(gsum_c)

    @pl.when(jnp.logical_not(has_next))
    def _():
        cbuf[...] = jnp.zeros_like(cbuf)
        gsum_a[...] = jnp.zeros_like(gsum_a)

    for ref in (acc_a, acc_b, acc_c, sum_a, sum_b, sum_c):
        ref[...] = jnp.zeros_like(ref)

    for c in loads:
        c.wait()

    as_int = lambda x: x.astype(jnp.int32)
    pl.semaphore_wait(barrier, width + as_int(has_prev) + as_int(has_next))

    def remote(src, dst, send, recv, device):
        return pltpu.make_async_remote_copy(
            src_ref=src, dst_ref=dst, send_sem=send, recv_sem=recv, device_id=device, device_id_type=MESH
        )

    ups = [remote(bbuf.at[q, core], abuf.at[q, core], up_send.at[q], a_recv.at[q], nxt) for q in range(n)]
    downs = [remote(bbuf.at[q, core], cbuf.at[q], down_send.at[q], c_recv.at[q], prev) for q in range(n)]
    fwds = [remote(abuf.at[q, core], abuf.at[q, core], fwd_send.at[q], fwd_recv.at[q], mate) for q in range(n)]
    shares = [remote(bbuf.at[q, core], bbuf.at[q, core], b_send.at[q], b_recv.at[q], mate) for q in range(n)]
    for c in shares:
        c.start()
    for q in range(n):
        @pl.when(has_next)
        def _(q=q):
            ups[q].start()

        @pl.when(has_prev)
        def _(q=q):
            downs[q].start()

    lane = lax.broadcasted_iota(jnp.int32, (1, k_all), 1)
    signs = jnp.where(lane < ks, -float(DT // DS), 1.0).astype(F32)
    signs_low = signs.astype(BF16)

    def half_norm(x):
        wide = x.astype(F32)
        return 0.5 * jnp.sum(wide * wide * signs, axis=1, keepdims=True)

    def as_row(col):
        m = col.shape[0]
        pieces = [
            jnp.transpose(jnp.broadcast_to(col[i : i + 128, 0:1], (128, 128)))[0:1, :] for i in range(0, m, 128)
        ]
        return pieces[0] if len(pieces) == 1 else jnp.concatenate(pieces, axis=1)

    def as_col(row):
        m = row.shape[1]
        pieces = [jnp.transpose(jnp.broadcast_to(row[0:1, i : i + 128], (128, 128))) for i in range(0, m, 128)]
        return pieces[0] if len(pieces) == 1 else jnp.concatenate(pieces, axis=0)

    def join(parts, axis):
        return parts[0] if len(parts) == 1 else jnp.concatenate(parts, axis=axis)

    scale = 2.0 / DT

    far_first = sorted(range(width - 1), key=lambda i: -min(i + 1, width - 1 - i))

    def scatter(i, src, dst):
        cs = [
            remote(src.at[peer(d)], dst.at[d - 1], rs_send.at[i, d - 1], rs_recv.at[i, d - 1], (me, peer(d)))
            for d in range(1, width)
        ]
        for i in far_first:
            cs[i].start()
        return cs

    def reduce(cs, src, dst, mask):
        total = src[wx].astype(F32)
        for c in cs:
            c.wait_recv()
        for d in range(width - 1):
            total = total + dst[d].astype(F32)
        if mask is not None:
            total = jnp.where(mask, total, 0.0)
        return total.astype(BF16)

    def gather(stage, out, low):
        out[wx] = low
        cs = [
            remote(out.at[wx], out.at[wx], ag_send.at[stage, d - 1], ag_recv.at[stage, d - 1], (me, peer(d)))
            for d in range(1, width)
        ]
        for i in far_first:
            cs[i].start()
        return cs

    scatters = [None] * (n + 1)
    gathers = [None] * (n + 1)

    half_o = []
    for q in range(n):
        shares[q].wait_recv()
        hb[:, q * both : (q + 1) * both] = as_row(half_norm(bbuf[q].reshape(both, k_all)))
        half_o.append(half_norm(bbuf[q, core]))
    mid, span = rows // 2, n // 2

    def half_block(ref, i, k, wide):
        return ref[pl.ds(i * span, span), k, :, 0:wide].reshape(mid, wide)

    match = [lax.rem(i + core, 2) for i in range(2)]

    def half_blocks(wide):
        own_halves = [half_block(bbuf, i, core, wide) for i in range(2)]
        return own_halves, [half_block(bbuf, match[i], other, wide) for i in range(2)]

    mine, theirs = half_blocks(k_all)
    norm_m = [half_norm(x) for x in mine]
    row_m = [as_row(x) for x in norm_m]
    row_t = [as_row(half_norm(x)) for x in theirs]
    pairs = [(0, mine[0], row_m[0]), (1, mine[0], row_m[0]), (1, mine[1], row_m[1])]
    pairs += [(0, theirs[0], row_t[0]), (1, theirs[1], row_t[1])]
    for i, (left, right, row) in enumerate(pairs):
        e = (dot(mine[left] * signs_low, right, 1, 1) - norm_m[left] - row) * scale
        eself[:, :, i * mid : (i + 1) * mid] = e.astype(BF16).reshape(width, mid // width, mid)
    scatters[0] = scatter(0, eself, eselfrecv)

    def view(ref, q, at, wide):
        return ref.at[q, :, :, pl.ds(at, wide)]

    def finish(stage):
        if stage == 0:
            gathers[0] = gather(0, rself, reduce(scatters[0], eself, eselfrecv, None))
            return
        q = stage - 1
        lanes = lax.broadcasted_iota(jnp.int32, (1, 2 * half), 1)
        with_b = lanes < both * (n - q)
        b_with_a = lanes >= half + both * (q + 1)
        far = jnp.logical_and(lax.rem(lanes // part, 2) == 0, core == 1)
        c_with_a = jnp.logical_and(jnp.logical_and(has_prev, has_next), jnp.logical_not(far))
        mask = jnp.where(
            with_b, as_int(has_next), jnp.where(b_with_a, as_int(has_prev), as_int(c_with_a))
        )
        gathers[stage] = []
        for h in range(2):
            cs = scatters[stage][h * (width - 1) : (h + 1) * (width - 1)]
            send, recv, out = [view(ref, q, h * half, half) for ref in (esend, erecv, rfull)]
            low = reduce(cs, send, recv, mask[:, h * half : (h + 1) * half] > 0)
            gathers[stage] += gather(1 + 2 * q + h, out, low)

    def row_sum(r):
        return jnp.broadcast_to(jnp.sum(r.astype(F32), axis=1, keepdims=True), (r.shape[0], 128))

    def col_sum(r):
        return jnp.sum(r.astype(F32), axis=0, keepdims=True)

    def pull(stage):
        for c in gathers[stage]:
            c.wait_recv()
        if stage == 0:
            r = rself[...].reshape(mid, 5 * mid)
            r00, r10, r11, x0, x1 = [r[:, i * mid : (i + 1) * mid] for i in range(5)]
            (s0, s1), (t0, t1) = half_blocks(ks)
            acc_o[0:span] = (dot(r00, s0, 1, 0) + dot(r10, s1, 0, 0) + dot(x0, t0, 1, 0)).reshape(span, part, ks)
            acc_o[span:n] = (dot(r10, s0, 1, 0) + dot(r11, s1, 1, 0) + dot(x1, t1, 1, 0)).reshape(span, part, ks)
            sum_o[0:span] = (row_sum(r00) + row_sum(x0) + as_col(col_sum(r10))).reshape(span, part, 128)
            sum_o[span:n] = (row_sum(r10) + row_sum(r11) + row_sum(x1)).reshape(span, part, 128)
            for i, (x, s_i) in enumerate([(x0, s0), (x1, s1)]):
                at = pl.ds(match[i] * span, span)
                acc_b[at, other] += dot(x, s_i, 0, 0).reshape(span, part, ks)
                msum_e[match[i]] = jnp.broadcast_to(col_sum(x), (8, mid))
            return
        q = stage - 1
        last = stage == n
        b_end = both * (n - q)
        r = rfull[q].reshape(part, 2 * half)
        rb, ra = r[:, 0:b_end], r[:, b_end:half]
        rs = join([r[:, half + both * i : half + both * (i + 1)] for i in range(n)], 0)
        sc = cbuf[q, :, 0:ks]
        sa = abuf[q, :, :, 0:ks].reshape(both, ks)
        left = [sc] + [cbuf[p, :, 0:ks] for p in range(q)] + [bbuf[p, core, :, 0:ks] for p in range(q + 1, n)]
        acc_a[q] += dot(rs, join(left, 0), 0, 0).reshape(2, part, ks)
        sum_a[0:1, both * q : both * (q + 1)] += col_sum(rs)
        if q:
            acc_a[0:q] += dot(ra, sc, 0, 0).reshape(q, 2, part, ks)
            sum_a[0:1, 0 : both * q] += col_sum(ra)
        if last:
            send_rows_a()
        x = dot(rs, sa, 1, 0)
        xs = row_sum(rs)
        y = dot(rb, bbuf[q:n, :, :, 0:ks].reshape(b_end, ks), 1, 0)
        if q:
            y += dot(ra, abuf[0:q, :, :, 0:ks].reshape(both * q, ks), 1, 0)
        acc_c[q] += x[0:part] + y
        sum_c[q] += xs[0:part] + row_sum(r[:, 0:half])
        if q:
            acc_c[0:q] += x[part : part * (q + 1)].reshape(q, part, ks)
            sum_c[0:q] += xs[part : part * (q + 1)].reshape(q, part, 128)
        if last:
            send_rows_c()
        acc_b[q:n] += dot(rb, sc, 0, 0).reshape(n - q, 2, part, ks)
        sum_b[0:1, both * q : half] += col_sum(rb)
        if last:
            send_rows_d()
        else:
            acc_o[q + 1 : n] += x[part * (q + 1) :].reshape(n - 1 - q, part, ks)
            sum_o[q + 1 : n] += xs[part * (q + 1) :].reshape(n - 1 - q, part, 128)

    def pair(i, src, dst, ssrc, sdst, device):
        return [
            remote(src, dst, m_send.at[2 * i], m_recv.at[2 * i], device),
            remote(ssrc, sdst, m_send.at[2 * i + 1], m_recv.at[2 * i + 1], device),
        ]

    send_c = pair(0, msg_c, got_c, msum_c, gsum_c, nxt)
    send_a = pair(1, msg_a, got_a, msum_a, gsum_a, prev)
    send_x = pair(2, msg_x, got_x, msum_x, gsum_x, mate)
    send_d = pair(3, msg_d, got_d, msum_d, gsum_d, mate)
    send_d.append(remote(msum_e, gsum_e, m_send.at[8], m_recv.at[8], mate))

    def begin(cs):
        for c in cs:
            c.start()

    def arrive(cs):
        for c in cs:
            c.wait_recv()

    def send_rows_a():
        @pl.when(has_prev)
        def _():
            msg_x[...] = acc_a[:, other].reshape(rows, ks)
            msum_x[...] = jnp.broadcast_to(sum_a[0:1], (8, half))
            begin(send_x)

    def send_rows_c():
        @pl.when(has_next)
        def _():
            msg_c[...] = acc_c[...].reshape(rows, ks).astype(BF16)
            begin(send_c[:1])
            msum_c[...] = jnp.broadcast_to(as_row(sum_c[...].reshape(rows, 128)), (8, rows))
            begin(send_c[1:])

        @pl.when(has_prev)
        def _():
            arrive(send_x)
            msg_a[...] = (acc_a[:, core].reshape(rows, ks) + got_x[...]).astype(BF16)
            begin(send_a[:1])
            msum_a[...] = jnp.broadcast_to(sum_a[0:1] + gsum_x[0:1], (8, half))
            begin(send_a[1:])

    def send_rows_d():
        msg_d[...] = acc_b[:, other].reshape(rows, ks)
        msum_d[...] = jnp.broadcast_to(sum_b[0:1], (8, half))
        begin(send_d)

    half_c, half_a = [], []
    for q in range(n):
        stage = 1 + q

        @pl.when(has_prev)
        def _(q=q):
            ups[q].wait_recv()
            fwds[q].start()

        @pl.when(has_next)
        def _(q=q):
            downs[q].wait_recv()

        half_c.append(half_norm(cbuf[q]))

        def put(at, tile):
            wide = tile.shape[1]
            esend[q, :, :, at : at + wide] = (tile * scale).astype(BF16).reshape(width, piece, wide)

        c_scaled = cbuf[q] * signs_low
        b_end = both * (n - q)
        put(0, dot(c_scaled, bbuf[q:n].reshape(b_end, k_all), 1, 1) - half_c[q] - hb[:, both * q : half])
        if q:
            g = dot(c_scaled, abuf[0:q].reshape(both * q, k_all), 1, 1)
            put(b_end, g - half_c[q] - join(half_a, 1))
        scatters[stage] = scatter(2 * q + 1, view(esend, q, 0, half), view(erecv, q, 0, half))

        @pl.when(has_prev)
        def _(q=q):
            fwds[q].wait_recv()

        a_q = abuf[q].reshape(both, k_all)
        half_a.append(as_row(half_norm(a_q)))
        left = [cbuf[q]] + [cbuf[p] for p in range(q)] + [bbuf[p, core] for p in range(q + 1, n)]
        norms = [half_c[q]] + half_c[0:q] + half_o[q + 1 : n]
        g = dot(join(left, 0) * signs_low, a_q, 1, 1)
        for i in range(n):
            put(half + both * i, g[part * i : part * (i + 1)] - norms[i] - half_a[q])
        scatters[stage] += scatter(2 * q + 2, view(esend, q, half, half), view(erecv, q, half, half))
        finish(stage - 1)
        if q > 1:
            pull(stage - 3)
    pull(n - 2)
    finish(n)
    pull(n - 1)
    pull(n)

    o_ref[...] = acc_b[:, core].reshape(rows, ks) + acc_o[...].reshape(rows, ks)
    arrive(send_d)
    o_ref[...] += got_d[...]

    @pl.when(has_prev)
    def _():
        arrive(send_c)
        o_ref[...] += got_c[...].astype(F32)

    @pl.when(has_next)
    def _():
        arrive(send_a)
        o_ref[...] += got_a[...].astype(F32)

    col_k[...] = as_col(gsum_a[0:1] + gsum_d[0:1] + sum_b[0:1]).reshape(n, 2, part, 128)
    total = as_col(gsum_c[0:1]) + col_k[:, core].reshape(rows, 128) + sum_o[...].reshape(rows, 128)
    total += join([as_col(gsum_e[i, 0:1]) for i in range(2)], 0)
    near = (2 * REACH + 1) * rows
    s_own = bbuf[:, core, :, 0:ks].reshape(rows, ks).astype(F32)
    for i in range(0, ks, 128):
        o_ref[:, i : i + 128] = (s_own[:, i : i + 128] * total - o_ref[:, i : i + 128]) * (1.0 / near)

    for cs in [shares, send_d] + scatters + gathers:
        for c in cs:
            c.wait_send()

    @pl.when(has_next)
    def _():
        for c in ups + send_c:
            c.wait_send()

    @pl.when(has_prev)
    def _():
        for c in downs + fwds + send_a + send_x:
            c.wait_send()


def solution(mesh):
    batch, width = mesh.shape["batch"], mesh.shape["width"]
    n = CHUNKS

    def body(teacher, student):
        rows, kt = teacher.shape
        ks = student.shape[1]
        part = rows // n
        k_all = ks + kt
        half = 2 * rows
        wide = 2 * half
        dma = pltpu.SemaphoreType.DMA
        low = lambda *shape: pltpu.VMEM(shape, BF16)
        full = lambda *shape: pltpu.VMEM(shape, F32)
        return pl.pallas_call(
            functools.partial(kernel, batch, width, rows, ks, kt, n),
            out_shape=jax.ShapeDtypeStruct((rows, ks), F32),
            in_specs=[pl.BlockSpec(memory_space=pl.ANY)] * 2,
            out_specs=pl.BlockSpec(memory_space=pltpu.VMEM),
            scratch_shapes=[
                low(n, 2, part, k_all), low(n, 2, part, k_all), low(n, part, k_all),
                low(width, rows // 2 // width, 5 * rows // 2), low(width, rows // 2 // width, 5 * rows // 2),
                low(n, width, part // width, wide), low(n, width - 1, part // width, wide),
                low(width - 1, rows // 2 // width, 5 * rows // 2), low(n, width, part // width, wide),
                full(n, 2, part, ks), full(n, 2, part, ks), full(n, part, ks), full(n, part, ks),
                full(8, half), full(8, half), full(n, part, 128), full(n, part, 128),
                low(rows, ks), low(rows, ks), full(rows, ks), full(rows, ks),
                full(8, rows), full(8, half), full(8, half), full(8, half),
                low(rows, ks), low(rows, ks), full(rows, ks), full(rows, ks),
                full(8, rows), full(8, half), full(8, half), full(8, half),
                full(2, 8, rows // 2), full(2, 8, rows // 2), full(1, half), full(n, 2, part, 128),
                dma((2 * n,)), dma((n,)), dma((n,)), dma((n,)), dma((n,)), dma((n,)), dma((n,)), dma((n,)), dma((n,)),
                dma((2 * n + 1, width - 1)), dma((2 * n + 1, width - 1)),
                dma((2 * n + 1, width - 1)), dma((2 * n + 1, width - 1)),
                dma((9,)), dma((9,)),
            ],
            compiler_params=pltpu.CompilerParams(
                collective_id=0, has_side_effects=True, vmem_limit_bytes=60 * 2**20
            ),
        )(teacher, student)

    specs = (P("batch", "width"), P("batch", "width"))
    return jax.shard_map(body, mesh=mesh, in_specs=specs, out_specs=P("batch", "width"), check_vma=False)
```
